512 devices in a mesh: dom: 64 (over z, x, core), slab: 8 (over y).
Axes of the slice: x: 4, y: 8, z: 8, core: 2. Of those that a mesh axis runs over, the one named last changes fastest.
Arguments:
- density_map: float32 [64, 512, 1024], P('dom', None, 'slab'), may hold values from 0.1 to 12
- offsets: float32 [3, 64, 8, 512], P(None, 'dom', 'slab'), may hold values from 0 to 1
- velocities: float32 [3, 64, 8, 512], P(None, 'dom', 'slab'), may hold values from -1.2 to 1.2
- weights: float32 [64, 8, 512], P('dom', 'slab'), may hold values from 1 to 16
- atom_cells: int32 [3, 64, 8, 512], P(None, 'dom', 'slab'), may hold values from 0 to 1020, as said below
- pair_tiles: int32 [64, 8, 2, 3], P('dom', 'slab'), may hold values from 0 to 3, as said below
- halo_lists: int32 [64, 8, 4, 128], P('dom', 'slab'), may hold values from 0 to 511, as said below
Outputs:
- displacement: float32 [3, 64, 8, 512], P(None, 'dom', 'slab')
- final_velocities: float32 [3, 64, 8, 512], P(None, 'dom', 'slab')
The draws below stay inside these ranges and needn't reach their ends.
Inputs may be any that keep to these rules, and one draw needn't show every extreme that they name: `atom_cells`: an atom of the device at dom index d and slab index s has x cell in [3, 61), y cell in [d * 8, (d + 1) * 8) and z cell in [s * 128 + 3, (s + 1) * 128 - 3). `pair_tiles`: row b of a device starts with b itself, then names distinct other source blocks; sources 2 and 3 are the rim atoms. `halo_lists`: each list holds 128 distinct atoms of the device.
All inputs are finite; a program needn't handle non-finite values.
Results may differ from the reference program's by a relative error of at most 0.017.
Values may be sent and summed in bfloat16 or wider, within the bound.
A program may use at most 128 MiB of HBM per device.

```python
import math
import jax
import jax.numpy as jnp
from jax import lax

REACH = 3
BLOCK = 256
BLOCKS = 2
TILES_PER = 3
DOMAIN_Y = 8
SLAB_Z = 128
STEPS = 3
ATOMS = 512
HALO = 128
ATOMS_ALL = 262144
NX = 64
NY = 512
NZ = 1024
N_DOM = 64
N_SLAB = 8


def draw_density_map(key, part):
    key = jax.random.fold_in(key, 11)
    ramp = jnp.exp(jnp.arange(NX, dtype=jnp.float32) * (math.log(4.0) / (NX - 1)))
    base = jnp.exp(jax.random.uniform(key, (NX, NY, NZ), jnp.float32, math.log(0.3), math.log(3.0)))
    return (base * ramp[:, None, None]).astype(jnp.float32)


def draw_atom_cells(key, part):
    key = jax.random.fold_in(key, 23)
    first_key, second_key, third_key = jax.random.split(key, 3)
    grid_shape = (N_DOM, N_SLAB, BLOCKS * BLOCK)
    x_cells = jax.random.randint(first_key, grid_shape, REACH, NX - REACH)
    dom_start = (jnp.arange(N_DOM, dtype=jnp.int32) * DOMAIN_Y)[:, None, None]
    y_cells = dom_start + jax.random.randint(second_key, grid_shape, 0, DOMAIN_Y)
    slab_start = (jnp.arange(N_SLAB, dtype=jnp.int32) * SLAB_Z)[None, :, None]
    z_cells = slab_start + jax.random.randint(third_key, grid_shape, REACH, SLAB_Z - REACH)
    return jnp.stack([x_cells, y_cells, z_cells]).astype(jnp.int32)


def draw_pair_tiles(key, part):
    key = jax.random.fold_in(key, 37)
    others = BLOCKS + 1
    scores = jax.random.randint(key, (N_DOM, N_SLAB, BLOCKS, others), 0, 1 << 20) * others + jnp.arange(others, dtype=jnp.int32)
    ranking = jnp.argsort(scores, axis=-1)[..., :TILES_PER - 1].astype(jnp.int32)
    itself = jnp.broadcast_to(jnp.arange(BLOCKS, dtype=jnp.int32)[None, None, :, None], (N_DOM, N_SLAB, BLOCKS, 1))
    picked = jnp.where(ranking < itself, ranking, ranking + 1)
    return jnp.concatenate([itself, picked], axis=-1).astype(jnp.int32)


def draw_halo_lists(key, part):
    key = jax.random.fold_in(key, 53)
    atom_count = BLOCKS * BLOCK
    scores = jax.random.randint(key, (N_DOM, N_SLAB, 4, atom_count), 0, 1 << 20) * atom_count + jnp.arange(atom_count, dtype=jnp.int32)
    return jnp.argsort(scores, axis=-1)[..., :HALO].astype(jnp.int32)


def steps_of(key, dims, shards, smallest, high):
    loudness = 1.0
    for axis_at, blocks in shards:
        steps = jax.random.uniform(jax.random.fold_in(jax.random.fold_in(key, 6), axis_at), (blocks,), jnp.float32, smallest / len(shards), high / len(shards))
        loudness = loudness * jnp.repeat(jnp.exp(steps), dims[axis_at] // blocks).reshape((-1,) + (1,) * (len(dims) - 1 - axis_at))
    return loudness


def normal_values(key, dims, deviation, most, shards=(), kind=jnp.bfloat16):
    gain = steps_of(key, dims, shards, -0.22, 0.18) if shards else 1.0
    result = jax.random.normal(key, dims, jnp.float32) * deviation * gain
    return jnp.minimum(jnp.maximum(result, -most), most).astype(kind)


def setup_inputs(seed: int = 0) -> dict:
    seeds = jax.random.split(jax.random.key(seed), 8)
    density_map = draw_density_map(jax.random.fold_in(seeds[7], 71), 0)
    offsets = jnp.clip(1.0 * jax.random.uniform(seeds[1], (3, N_DOM, N_SLAB, ATOMS), jnp.float32) ** steps_of(seeds[1], (3, N_DOM, N_SLAB, ATOMS), ((1, 64), (2, 8)), -0.2, 0.2), 0.0, 1.0)
    velocities = normal_values(seeds[2], (3, N_DOM, N_SLAB, ATOMS), 0.2, 1.2, ((1, 64), (2, 8)), jnp.float32)
    weights = jnp.clip(jnp.exp(math.log(16.0) - 2.7725887 * jax.random.uniform(seeds[3], (N_DOM, N_SLAB, ATOMS), jnp.float32) ** steps_of(seeds[3], (N_DOM, N_SLAB, ATOMS), ((0, 64), (1, 8)), -0.2, 0.2)), 1.0, 16.0)
    atom_cells = draw_atom_cells(jax.random.fold_in(seeds[7], 71), 0)
    pair_tiles = draw_pair_tiles(jax.random.fold_in(seeds[7], 71), 0)
    halo_lists = draw_halo_lists(jax.random.fold_in(seeds[7], 71), 0)
    return dict(density_map=density_map, offsets=offsets, velocities=velocities, weights=weights, atom_cells=atom_cells, pair_tiles=pair_tiles, halo_lists=halo_lists)


FORCE_GAIN = 2.0
PAIR_GAIN = 0.1
PAIR_SOFT = 64.0
TIME_STEP = 0.25

def stencil_rows(offset, reach):
    spacing = (jnp.arange(2 * reach + 1) - reach).astype(jnp.float32)[:, None] - offset[None, :]
    values = jnp.exp(-0.5 * spacing * spacing)
    return (values, values * spacing)

def expand_rows(values, first, length):
    relative = jnp.arange(length, dtype=jnp.int32)[:, None] - first[None, :].astype(jnp.int32)
    total = jnp.zeros((length, values.shape[1]), jnp.float32)
    for offset_index in range(values.shape[0]):
        total = total + jnp.where(relative == offset_index, values[offset_index][None, :], jnp.float32(0.0))
    return total

def atom_factors(moved, cells, x_first, x_length, y_cells, z_cells, reach):
    x_vals, x_slopes = stencil_rows(moved[0], reach)
    y_vals, y_slopes = stencil_rows(moved[1], reach)
    z_vals, z_slopes = stencil_rows(moved[2], reach)
    x_start = cells[0] - reach - x_first
    y_start = cells[1] % y_cells
    z_start = cells[2] % z_cells - reach
    x_factors = jnp.concatenate([expand_rows(x_vals, x_start, x_length), expand_rows(x_slopes, x_start, x_length)], axis=1).astype(jnp.bfloat16)
    y_width = y_cells + 2 * reach
    y_parts = (expand_rows(y_vals, y_start, y_width), expand_rows(y_slopes, y_start, y_width))
    z_parts = (expand_rows(z_vals, z_start, z_cells), expand_rows(z_slopes, z_start, z_cells))
    return (x_factors, y_parts, z_parts)

def spread_block(x_factors, y_parts, z_parts, weights):
    count = weights.shape[0]
    cross = (weights[None, None, :] * y_parts[0][:, None, :] * z_parts[0][None, :, :]).astype(jnp.bfloat16)
    cross = cross.reshape(-1, count)
    return lax.dot_general(x_factors[:, :count], cross, (((1,), (1,)), ((), ())), preferred_element_type=jnp.float32)

def pull_block(window, x_factors, y_parts, z_parts, weights):
    count = weights.shape[0]
    pulled = lax.dot_general(window, x_factors, (((0,), (0,)), ((), ())), preferred_element_type=jnp.float32)
    pulled = pulled.reshape(y_parts[0].shape[0], z_parts[0].shape[0], 2 * count)
    plain = pulled[:, :, :count]
    sloped = pulled[:, :, count:]
    plain_z = lax.optimization_barrier(jnp.sum(plain * z_parts[0][None], axis=1))
    sloped_z = lax.optimization_barrier(jnp.sum(sloped * z_parts[0][None], axis=1))
    plain_dz = lax.optimization_barrier(jnp.sum(plain * z_parts[1][None], axis=1))
    force_x = lax.optimization_barrier(jnp.sum(sloped_z * y_parts[0], axis=0))
    force_y = lax.optimization_barrier(jnp.sum(plain_z * y_parts[1], axis=0))
    force_z = lax.optimization_barrier(jnp.sum(plain_dz * y_parts[0], axis=0))
    return weights[None, :] * jnp.stack([force_x, force_y, force_z])

def pair_block_forces(targets, target_weights, sources, source_weights, tiles, block):
    results = []
    for block_index in range(tiles.shape[0]):
        near = targets[:, block_index * block:(block_index + 1) * block]
        near_weights = target_weights[block_index * block:(block_index + 1) * block]
        total = jnp.zeros((3, block), jnp.float32)
        for tile_index in range(tiles.shape[1]):
            start = tiles[block_index, tile_index].astype(jnp.int32) * block
            far = lax.dynamic_slice_in_dim(sources, start, block, 1)
            far_weights = lax.dynamic_slice_in_dim(source_weights, start, block, 0)
            between = near[:, :, None] - far[:, None, :]
            squared = lax.optimization_barrier(jnp.sum(between * between, axis=0)) + PAIR_SOFT
            falloff = far_weights[None, :] / (squared * jnp.sqrt(squared))
            total = total + lax.optimization_barrier(jnp.sum(between * falloff[None], axis=2))
        results.append(PAIR_GAIN * near_weights[None, :] * total)
    return jnp.concatenate(results, axis=1)

def from_lower(array, axis):
    empty = jnp.zeros_like(lax.slice_in_dim(array, 0, 1, axis=axis))
    return jnp.concatenate([empty, lax.slice_in_dim(array, 0, array.shape[axis] - 1, axis=axis)], axis=axis)

def from_upper(array, axis):
    empty = jnp.zeros_like(lax.slice_in_dim(array, 0, 1, axis=axis))
    return jnp.concatenate([lax.slice_in_dim(array, 1, array.shape[axis], axis=axis), empty], axis=axis)

def reference(density_map, offsets, velocities, weights, atom_cells, pair_tiles, halo_lists):
    count = N_DOM * N_SLAB
    y_width = DOMAIN_Y + 2 * REACH
    scale = FORCE_GAIN * math.sqrt(float(NX * NY * NZ * ATOMS_ALL))
    cells = atom_cells.reshape(3, count, ATOMS)
    weight_flat = weights.reshape(count, ATOMS)
    tiles = pair_tiles.reshape(count, BLOCKS, TILES_PER)
    base = offsets.reshape(3, count, ATOMS)
    speed = velocities.reshape(3, count, ATOMS)
    shifted = jnp.zeros((3, count, ATOMS), jnp.float32)
    map_square = jnp.sum(density_map * density_map)
    indices = jnp.arange(count, dtype=jnp.int32)
    zero_index = jnp.zeros((), jnp.int32)
    for step_index in range(STEPS):
        moved = base + shifted

        def add_partial(index, padded):
            index = jnp.asarray(index).astype(jnp.int32)
            local_moved = moved[:, index]
            local_cells = cells[:, index]
            local_weights = weight_flat[index]
            partial_value = jnp.zeros((NX, y_width * SLAB_Z), jnp.float32)
            for block_index in range(BLOCKS):
                lower = block_index * BLOCK
                factors = atom_factors(local_moved[:, lower:lower + BLOCK], local_cells[:, lower:lower + BLOCK], 0, NX, DOMAIN_Y, SLAB_Z, REACH)
                partial_value = partial_value + spread_block(factors[0], factors[1], factors[2], local_weights[lower:lower + BLOCK])
            partial_value = partial_value.reshape(NX, y_width, SLAB_Z)
            place = (zero_index, index // N_SLAB * DOMAIN_Y, index % N_SLAB * SLAB_Z)
            current = lax.dynamic_slice(padded, place, partial_value.shape)
            return lax.dynamic_update_slice(padded, current + partial_value, place)
        padded = lax.fori_loop(0, count, add_partial, jnp.zeros((NX, NY + 2 * REACH, NZ), jnp.float32))
        rho = padded[:, REACH:REACH + NY]
        cross_sum = jnp.sum(rho * density_map)
        rho_square = jnp.sum(rho * rho)
        norm = jnp.sqrt(rho_square * map_square)
        gradient = (density_map / norm - rho * (cross_sum / (norm * rho_square))).astype(jnp.bfloat16)
        padded_gradient = jnp.pad(gradient, ((0, 0), (REACH, REACH), (0, 0)))

        def device_force(index):
            place = (zero_index, index // N_SLAB * DOMAIN_Y, index % N_SLAB * SLAB_Z)
            window = lax.dynamic_slice(padded_gradient, place, (NX, y_width, SLAB_Z)).reshape(NX, y_width * SLAB_Z)
            local_moved = moved[:, index]
            local_cells = cells[:, index]
            local_weights = weight_flat[index]
            pieces = []
            for block_index in range(BLOCKS):
                lower = block_index * BLOCK
                factors = atom_factors(local_moved[:, lower:lower + BLOCK], local_cells[:, lower:lower + BLOCK], 0, NX, DOMAIN_Y, SLAB_Z, REACH)
                pieces.append(pull_block(window, factors[0], factors[1], factors[2], local_weights[lower:lower + BLOCK]))
            return jnp.concatenate(pieces, axis=1)
        density_force = jnp.transpose(lax.map(device_force, indices), (1, 0, 2))
        positions = cells.astype(jnp.float32) + moved
        grid_positions = positions.reshape(3, N_DOM, N_SLAB, ATOMS)
        grid_weights = weight_flat.reshape(N_DOM, N_SLAB, ATOMS)
        sent_positions = [jnp.take_along_axis(grid_positions, halo_lists[None, :, :, entry, :], axis=3) for entry in range(4)]
        sent_weights = [jnp.take_along_axis(grid_weights, halo_lists[:, :, entry, :], axis=2) for entry in range(4)]
        sources = jnp.concatenate([grid_positions, from_lower(sent_positions[1], 1), from_upper(sent_positions[0], 1), from_lower(sent_positions[3], 2), from_upper(sent_positions[2], 2)], axis=3)
        source_weights = jnp.concatenate([grid_weights, from_lower(sent_weights[1], 0), from_upper(sent_weights[0], 0), from_lower(sent_weights[3], 1), from_upper(sent_weights[2], 1)], axis=2)
        flat_sources = sources.reshape(3, count, -1)
        flat_source_weights = source_weights.reshape(count, -1)

        def device_pair(index):
            return pair_block_forces(positions[:, index], weight_flat[index], flat_sources[:, index], flat_source_weights[index], tiles[index], BLOCK)
        pair_force = jnp.transpose(lax.map(device_pair, indices), (1, 0, 2))
        force = scale * density_force + pair_force
        speed = speed + TIME_STEP * force
        shifted = shifted + TIME_STEP * speed
    return (shifted.reshape(3, N_DOM, N_SLAB, ATOMS), speed.reshape(3, N_DOM, N_SLAB, ATOMS))
```

```python
import functools
import math

import jax
import jax.numpy as jnp
from jax import lax
from jax.experimental import pallas as pl
from jax.experimental.pallas import tpu as pltpu
from jax.sharding import PartitionSpec as P

REACH = 3
BLOCK = 256
BLOCKS = 2
TILES_PER = 3
STEPS = 3
ATOMS = 512
HALO = 128
DOMAINS = 64
SLABS = 8
X_CELLS = 64
Y_CELLS = 8
Z_CELLS = 128
ROWS = 16
BELOW = 4
Z_CHIPS, X_CHIPS, CORES = 8, 4, 2

FORCE_GAIN = 2.0
PAIR_GAIN = 0.1
PAIR_SOFT = 64.0
TIME_STEP = 0.25
SCALE = FORCE_GAIN * math.sqrt(float(X_CELLS * Y_CELLS * DOMAINS * Z_CELLS * SLABS * ATOMS * DOMAINS * SLABS))

MESH = pl.DeviceIdType.MESH
F32, BF16 = jnp.float32, jnp.bfloat16
BASE, U, V, CELL, WEIGHT, RECORD = 0, 3, 6, 9, 12, 16
LOWER, UPPER = 0, 1


def for_dom_peers(dom, do):
    z, x, core = dom // (X_CHIPS * CORES), dom // CORES % X_CHIPS, dom % CORES

    def along_x(dz):
        for dx in (2, 1, 3, 0):
            for dc in (1, 0):
                if isinstance(dz, int) and dz + dx + dc == 0:
                    continue
                peer = ((z + dz) % Z_CHIPS * X_CHIPS + (x + dx) % X_CHIPS) * CORES + (core + dc) % CORES
                do((dz * X_CHIPS + dx) * CORES + dc - 1, peer)

    def body(j, carry):
        along_x(Z_CHIPS // 2 + (1 - 2 * (j % 2)) * ((j + 1) // 2))
        return carry

    lax.fori_loop(0, Z_CHIPS - 1, body, 0)
    along_x(0)


def for_slab_peers(slab, do):
    for k in (4, 3, 5, 2, 6, 1, 7):
        do(k - 1, (slab + k) % SLABS)


def total_of(ref, count):
    sums = []
    for first in range(0, count, 16):
        sums.append(jnp.sum(ref[first : min(first + 16, count)], axis=0))
    return functools.reduce(jnp.add, sums)


def stencil(cell, moved, index):
    steps = index - cell
    spacing = steps - moved
    values = jnp.where(jnp.abs(steps) <= float(REACH), jnp.exp(-0.5 * spacing * spacing), 0.0)
    return values, values * spacing


def float_iota(shape, dim):
    return lax.broadcasted_iota(jnp.int32, shape, dim).astype(F32)


def kernel(
    map_ref, offsets_ref, velocities_ref, weights_ref, cells_ref, tiles_ref, lists_ref,
    moved_out, speed_out,
    padded, map_send, map_recv, map_rows, windows, rho,
    records, record_recv, xf_pair, xf_pull, y_own, ys_own, y_near, z_near, zs_own,
    one_hot, rim_send, rim_recv, sources, state, pulls, ab, map_square,
    sums_send, dom_recv, slab_send, slab_recv,
    map_ssem, map_rsem, rec_ssem, rec_rsem, rim_ssem, rim_rsem, dom_ssem, dom_rsem, slab_ssem, slab_rsem,
):
    dom, slab = lax.axis_index("dom"), lax.axis_index("slab")
    lower, upper = (dom + DOMAINS - 1) % DOMAINS, (dom + 1) % DOMAINS
    before, after = (slab + SLABS - 1) % SLABS, (slab + 1) % SLABS

    barrier = pltpu.get_barrier_semaphore()

    def greet(k, carry):
        pl.semaphore_signal(barrier, inc=1, device_id=((dom + k) % DOMAINS, slab), device_id_type=MESH)
        return carry

    lax.fori_loop(1, DOMAINS, greet, 0)
    for k in range(1, SLABS):
        pl.semaphore_signal(barrier, inc=1, device_id=(dom, (slab + k) % SLABS), device_id_type=MESH)

    padded[0:8] = jnp.zeros((8, Z_CELLS), F32)
    padded[512:520] = jnp.zeros((8, Z_CELLS), F32)
    own_map = map_ref[0]
    padded[BELOW : BELOW + 512] = own_map
    square = own_map * own_map
    square = jnp.sum(jnp.sum(square.reshape(64, 8, Z_CELLS), axis=0), axis=0, keepdims=True)
    map_square[...] = square + pltpu.roll(square, 64, 1)

    def cut(t, carry):
        first = pl.multiple_of(t * Y_CELLS, Y_CELLS)
        map_send[t] = padded[pl.ds(first, ROWS)].astype(BF16)
        return carry

    lax.fori_loop(0, DOMAINS, cut, 0, unroll=8)
    map_recv[dom] = map_send[dom]

    weights = weights_ref[0]
    zero_row = jnp.zeros((1, ATOMS), F32)
    cell_rows = [cells_ref[i, 0].astype(F32) for i in range(3)]
    local_rows = [
        cell_rows[0],
        (cells_ref[1, 0] - dom * Y_CELLS).astype(F32),
        (cells_ref[2, 0] - slab * Z_CELLS).astype(F32),
    ]
    offset_rows = [offsets_ref[i, 0] for i in range(3)]
    fixed = local_rows + [weights] + [zero_row] * (RECORD - WEIGHT - 1)
    records[0] = jnp.concatenate(offset_rows + [zero_row] * 6 + fixed, axis=0)
    for i in range(3):
        state[i : i + 1] = zero_row
        state[3 + i : 4 + i] = velocities_ref[i, 0]
    ab[...] = jnp.zeros((8, ATOMS), F32)
    atom_index = lax.broadcasted_iota(jnp.int32, (ATOMS, HALO), 0)
    for entry in range(4):
        one_hot[:, entry * HALO : (entry + 1) * HALO] = jnp.where(
            atom_index == lists_ref[0, 0, entry : entry + 1, :], 1.0, 0.0
        ).astype(BF16)

    pl.semaphore_wait(barrier, DOMAINS - 1 + SLABS - 1)

    def record_copy(step, slot, peer):
        return pltpu.make_async_remote_copy(
            src_ref=records.at[step],
            dst_ref=record_recv.at[step, slot],
            send_sem=rec_ssem.at[step, slot],
            recv_sem=rec_rsem.at[step, slot],
            device_id=(peer, slab),
            device_id_type=MESH,
        )

    def send_records(step):
        record_copy(step, UPPER, lower).start()
        record_copy(step, LOWER, upper).start()

    send_records(0)

    def send_map(slot, peer):
        pltpu.make_async_remote_copy(
            src_ref=map_send.at[peer],
            dst_ref=map_recv.at[dom],
            send_sem=map_ssem,
            recv_sem=map_rsem,
            device_id=(peer, slab),
            device_id_type=MESH,
        ).start()

    for_dom_peers(dom, send_map)

    def step_body(step, carry):
        a_row, b_row = ab[0:1], ab[1:2]
        record_copy(step, LOWER, upper).wait_recv()
        record_copy(step, UPPER, lower).wait_recv()

        row = lax.broadcasted_iota(jnp.int32, (ROWS, ATOMS), 0)
        first_row = jnp.where(dom == 0, BELOW, 0)
        last_row = jnp.where(dom == DOMAINS - 1, BELOW + Y_CELLS, ROWS)
        in_grid = (row >= first_row) & (row < last_row)
        y_index = row.astype(F32) - float(BELOW)
        x_index = float_iota((X_CELLS, ATOMS), 0)
        z_index = float_iota((Z_CELLS, ATOMS), 0)
        own_moved = []
        for kind in range(3):
            record = records[step] if kind == 0 else record_recv[step, kind - 1]
            moved = [
                record[BASE + i : BASE + i + 1]
                + a_row * record[U + i : U + i + 1]
                + b_row * record[V + i : V + i + 1]
                for i in range(3)
            ]
            cell = [record[CELL + i : CELL + i + 1] for i in range(3)]
            heavy = record[WEIGHT : WEIGHT + 1]
            xv, xs = stencil(cell[0], moved[0], x_index)
            shift = (0.0, -float(Y_CELLS), float(Y_CELLS))[kind]
            yv, ys = stencil(cell[1] + shift, moved[1], y_index)
            zv, zs = stencil(cell[2], moved[2], z_index)
            xv = xv.astype(BF16)
            z_near[kind] = zv
            if kind == 0:
                xf_pair[0, :, 0:ATOMS] = xv
                xf_pair[1, :, 0:ATOMS] = xv
                xf_pull[:, 0:ATOMS] = xv
                xf_pull[:, ATOMS:] = xs.astype(BF16)
                zs_own[...] = zs
                y_own[...] = jnp.where(in_grid, heavy * yv, 0.0)
                ys_own[...] = heavy * ys
            else:
                xf_pair[kind - 1, :, ATOMS:] = xv
                there = (dom > 0) if kind == 1 else (dom < DOMAINS - 1)
                y_near[kind - 1] = jnp.where(in_grid & there, heavy * yv, 0.0)
            if kind == 0:
                own_moved = moved

        def spread_half(half, carry):
            def spread_row(i, carry):
                r = 1 + half * 7 + i
                cross = jnp.concatenate(
                    [
                        (y_own[pl.ds(r, 1)] * z_near[0]).astype(BF16),
                        (y_near[half, pl.ds(r, 1)] * z_near[half + 1]).astype(BF16),
                    ],
                    axis=1,
                )
                out = lax.dot_general(cross, xf_pair[half], (((1,), (1,)), ((), ())), preferred_element_type=F32)
                place = pl.ds(pl.multiple_of(r * Z_CELLS, Z_CELLS), Z_CELLS)
                rho[place] = out
                windows[1, place] = out.astype(BF16)
                return carry

            return lax.fori_loop(0, 7, spread_row, carry)

        lax.fori_loop(0, 2, spread_half, 0)

        @pl.when(step == 0)
        def _():
            everything = map_recv.at[pl.ds(0, DOMAINS - 1)]
            pltpu.make_async_copy(everything, everything, map_rsem).wait()
            map_rows[...] = map_recv[...].astype(F32).reshape(X_CELLS * ROWS, Z_CELLS)

            for r in range(ROWS):
                plane = map_rows[pl.ds(r, X_CELLS, stride=ROWS)]
                windows[0, r * Z_CELLS : (r + 1) * Z_CELLS] = plane.T.astype(BF16)

        def sum_row(r, carry):
            rr, rm = carry
            place = pl.ds(pl.multiple_of(r * Z_CELLS, Z_CELLS), Z_CELLS)
            here = rho[place].reshape(16, 8, X_CELLS)
            there = windows[0, place].astype(F32).reshape(16, 8, X_CELLS)
            return rr + jnp.sum(here * here, axis=0), rm + jnp.sum(here * there, axis=0)

        nothing = jnp.zeros((8, X_CELLS), F32)
        rr, rm = lax.fori_loop(BELOW, BELOW + Y_CELLS, sum_row, (nothing, nothing))
        both = jnp.concatenate(
            [jnp.sum(rr, axis=0, keepdims=True), jnp.sum(rm, axis=0, keepdims=True)], axis=1
        )
        both = both + pltpu.roll(both, 96, 1)
        lane = lax.broadcasted_iota(jnp.int32, (1, 128), 1)
        sums = jnp.where(lane < 64, both, map_square[...])
        sums_send[step] = jnp.where((lane >= 32) & (lane < 64), pltpu.roll(both, 96, 1), sums)

        def dom_copy(slot, peer):
            pltpu.make_async_remote_copy(
                src_ref=sums_send.at[step],
                dst_ref=dom_recv.at[step, slot],
                send_sem=dom_ssem.at[step],
                recv_sem=dom_rsem.at[step],
                device_id=(peer, slab),
                device_id_type=MESH,
            ).start()

        for_dom_peers(dom, dom_copy)

        positions = jnp.concatenate([cell_rows[i] + own_moved[i] for i in range(3)] + [weights] + [zero_row] * 4, axis=0)
        high = positions.astype(BF16).astype(F32)
        middle = (positions - high).astype(BF16).astype(F32)
        low = positions - high - middle
        split = jnp.concatenate([high, middle, low, jnp.zeros((8, ATOMS), F32)], axis=0).astype(BF16)
        listed = jnp.dot(split, one_hot[...], preferred_element_type=F32)
        listed = listed[0:8] + listed[8:16] + listed[16:24]

        def rim_copy(entry):
            slot, place = (
                (1, (lower, slab)), (0, (upper, slab)), (3, (dom, before)), (2, (dom, after)),
            )[entry]
            return pltpu.make_async_remote_copy(
                src_ref=rim_send.at[step, entry],
                dst_ref=rim_recv.at[step, slot],
                send_sem=rim_ssem.at[step, entry],
                recv_sem=rim_rsem.at[step, slot],
                device_id=place,
                device_id_type=MESH,
            )

        for entry in range(4):
            rim_send[step, entry] = listed[:, entry * HALO : (entry + 1) * HALO]
            rim_copy(entry).start()

        def pull(which, carry):
            def pull_row(r, sums):
                place = pl.ds(pl.multiple_of(r * Z_CELLS, Z_CELLS), Z_CELLS)
                window = windows[which, place]
                yv, ys = y_own[pl.ds(r, 1)], ys_own[pl.ds(r, 1)]
                out = []
                for half in range(2):
                    at = slice(half * 256, (half + 1) * 256)
                    plain = jnp.dot(window, xf_pull[:, half * 256 : (half + 1) * 256], preferred_element_type=F32)
                    sloped = jnp.dot(window, xf_pull[:, ATOMS + half * 256 : ATOMS + (half + 1) * 256], preferred_element_type=F32)
                    zv, zs = z_near[0, :, at], zs_own[:, at]

                    def over_z(product):
                        return jnp.sum(product.reshape(16, 8, 256), axis=0)

                    out.append(sums[half * 3] + over_z(sloped * zv) * yv[:, at])
                    out.append(sums[half * 3 + 1] + over_z(plain * zv) * ys[:, at])
                    out.append(sums[half * 3 + 2] + over_z(plain * zs) * yv[:, at])
                return tuple(out)

            sums = lax.fori_loop(1, ROWS - 1, pull_row, (jnp.zeros((8, 256), F32),) * 6)
            for half in range(2):
                rows = [jnp.sum(sums[half * 3 + i], axis=0, keepdims=True) for i in range(3)]
                pulls[which, :, half * 256 : (half + 1) * 256] = jnp.concatenate(rows + [jnp.zeros((5, 256), F32)], axis=0)
            return carry

        lax.fori_loop(0, 2, pull, 0)

        rims = []
        for slot in range(4):
            rim_copy((1, 0, 3, 2)[slot]).wait_recv()
            there = ((dom > 0), (dom < DOMAINS - 1), (slab > 0), (slab < SLABS - 1))[slot]
            keep = (lax.broadcasted_iota(jnp.int32, (8, HALO), 0) != 3) | there
            rims.append(jnp.where(keep, rim_recv[step, slot], 0.0))
        blocks = [positions[:, 0:BLOCK], positions[:, BLOCK:]]
        blocks += [jnp.concatenate(rims[0:2], axis=1), jnp.concatenate(rims[2:4], axis=1)]
        for block in range(BLOCKS):
            for j in range(TILES_PER):
                listed_block = blocks[block]
                if j > 0:
                    source = jnp.full((8, BLOCK), tiles_ref[0, 0, block, j], jnp.int32)
                    listed_block = blocks[3]
                    for t in range(3):
                        listed_block = jnp.where(source == t, blocks[t], listed_block)
                sources[block, j * BLOCK : (j + 1) * BLOCK] = listed_block.T
        pair_rows = []
        for block in range(BLOCKS):
            at = slice(block * BLOCK, (block + 1) * BLOCK)
            near = [positions[i : i + 1, at] for i in range(3)]

            def chunk(c, total, block=block, near=near):
                far = sources[block, pl.ds(pl.multiple_of(c * 32, 32), 32)]
                between = [near[i] - far[:, i : i + 1] for i in range(3)]
                squared = between[0] * between[0] + between[1] * between[1] + between[2] * between[2] + PAIR_SOFT
                inverse = lax.rsqrt(squared)
                falloff = far[:, 3:4] * (inverse * inverse * inverse)
                return tuple(
                    total[i] + jnp.sum((between[i] * falloff).reshape(4, 8, BLOCK), axis=0) for i in range(3)
                )

            total = lax.fori_loop(0, TILES_PER * BLOCK // 32, chunk, (jnp.zeros((8, BLOCK), F32),) * 3)
            pair_rows.append([jnp.sum(t, axis=0, keepdims=True) for t in total])

        gain = TIME_STEP * TIME_STEP * SCALE
        u_rows, v_rows, base_rows = [], [], []
        for i in range(3):
            pair = jnp.concatenate([pair_rows[block][i] for block in range(BLOCKS)], axis=1)
            speed = state[3 + i : 4 + i] + TIME_STEP * (PAIR_GAIN * weights * pair)
            state[3 + i : 4 + i] = speed
            base_rows.append(own_moved[i] + TIME_STEP * speed)
            u_rows.append(gain * pulls[0, i : i + 1])
            v_rows.append(-gain * pulls[1, i : i + 1])
        record = jnp.concatenate(base_rows + u_rows + v_rows + fixed, axis=0)

        @pl.when(step < STEPS - 1)
        def _():
            records[step + 1] = record
            send_records(step + 1)

        pltpu.make_async_copy(dom_recv.at[step], dom_recv.at[step], dom_rsem.at[step]).wait()
        slab_send[step] = sums_send[step] + total_of(dom_recv.at[step], DOMAINS - 1)

        def slab_copy(slot, peer):
            pltpu.make_async_remote_copy(
                src_ref=slab_send.at[step],
                dst_ref=slab_recv.at[step, slot],
                send_sem=slab_ssem.at[step],
                recv_sem=slab_rsem.at[step],
                device_id=(dom, peer),
                device_id_type=MESH,
            ).start()

        for_slab_peers(slab, slab_copy)
        pltpu.make_async_copy(slab_recv.at[step], slab_recv.at[step], slab_rsem.at[step]).wait()
        sums = slab_send[step] + total_of(slab_recv.at[step], SLABS - 1)
        srr = jnp.sum(jnp.where(lane < 32, sums, 0.0), axis=1, keepdims=True)
        srm = jnp.sum(jnp.where((lane >= 32) & (lane < 64), sums, 0.0), axis=1, keepdims=True)
        smm = jnp.sum(jnp.where(lane >= 64, sums, 0.0), axis=1, keepdims=True)
        norm = jnp.sqrt(srr * smm)
        a = 1.0 / norm
        b = srm / (norm * srr)
        ab[0:1] = jnp.broadcast_to(a, (1, ATOMS))
        ab[1:2] = jnp.broadcast_to(b, (1, ATOMS))
        for i in range(3):
            speed = state[3 + i : 4 + i] + (a * u_rows[i] + b * v_rows[i]) * (1.0 / TIME_STEP)
            state[3 + i : 4 + i] = speed
            state[i : i + 1] = state[i : i + 1] + TIME_STEP * speed
        return carry

    lax.fori_loop(0, STEPS, step_body, 0)
    for i in range(3):
        moved_out[i, 0] = state[i : i + 1]
        speed_out[i, 0] = state[3 + i : 4 + i]

    everything = map_send.at[pl.ds(0, DOMAINS - 1)]
    pltpu.make_async_copy(everything, everything, map_ssem).wait()

    def drain(step, carry):
        record_copy(step, UPPER, lower).wait_send()
        record_copy(step, LOWER, upper).wait_send()
        for entry in range(4):
            pltpu.make_async_copy(rim_send.at[step, entry], rim_send.at[step, entry], rim_ssem.at[step, entry]).wait()
        pltpu.make_async_copy(dom_recv.at[step], dom_recv.at[step], dom_ssem.at[step]).wait()
        pltpu.make_async_copy(slab_recv.at[step], slab_recv.at[step], slab_ssem.at[step]).wait()
        return carry

    lax.fori_loop(0, STEPS, drain, 0)


def per_device(density_map, offsets, velocities, weights, atom_cells, pair_tiles, halo_lists):
    vmem = pl.BlockSpec(memory_space=pltpu.VMEM)
    smem = pl.BlockSpec(memory_space=pltpu.SMEM)
    out = jax.ShapeDtypeStruct(offsets.shape, F32)
    dma = pltpu.SemaphoreType.DMA
    scratch = [
        pltpu.VMEM((520, Z_CELLS), F32),
        pltpu.VMEM((DOMAINS, ROWS, Z_CELLS), BF16),
        pltpu.VMEM((X_CELLS, ROWS, Z_CELLS), BF16),
        pltpu.VMEM((X_CELLS * ROWS, Z_CELLS), F32),
        pltpu.VMEM((2, ROWS * Z_CELLS, X_CELLS), BF16),
        pltpu.VMEM((ROWS * Z_CELLS, X_CELLS), F32),
        pltpu.VMEM((STEPS, RECORD, ATOMS), F32),
        pltpu.VMEM((STEPS, 2, RECORD, ATOMS), F32),
        pltpu.VMEM((2, X_CELLS, 2 * ATOMS), BF16),
        pltpu.VMEM((X_CELLS, 2 * ATOMS), BF16),
        pltpu.VMEM((ROWS, ATOMS), F32),
        pltpu.VMEM((ROWS, ATOMS), F32),
        pltpu.VMEM((2, ROWS, ATOMS), F32),
        pltpu.VMEM((3, Z_CELLS, ATOMS), F32),
        pltpu.VMEM((Z_CELLS, ATOMS), F32),
        pltpu.VMEM((ATOMS, 4 * HALO), BF16),
        pltpu.VMEM((STEPS, 4, 8, HALO), F32),
        pltpu.VMEM((STEPS, 4, 8, HALO), F32),
        pltpu.VMEM((BLOCKS, TILES_PER * BLOCK, 8), F32),
        pltpu.VMEM((8, ATOMS), F32),
        pltpu.VMEM((2, 8, ATOMS), F32),
        pltpu.VMEM((8, ATOMS), F32),
        pltpu.VMEM((1, 128), F32),
        pltpu.VMEM((STEPS, 1, 128), F32),
        pltpu.VMEM((STEPS, DOMAINS - 1, 1, 128), F32),
        pltpu.VMEM((STEPS, 1, 128), F32),
        pltpu.VMEM((STEPS, SLABS - 1, 1, 128), F32),
        dma, dma,
        dma((STEPS, 2)), dma((STEPS, 2)),
        dma((STEPS, 4)), dma((STEPS, 4)),
        dma((STEPS,)), dma((STEPS,)),
        dma((STEPS,)), dma((STEPS,)),
    ]
    return pl.pallas_call(
        kernel,
        out_shape=(out, out),
        in_specs=[vmem, vmem, vmem, vmem, vmem, smem, vmem],
        out_specs=(vmem, vmem),
        scratch_shapes=scratch,
        compiler_params=pltpu.CompilerParams(
            collective_id=0, has_side_effects=True, vmem_limit_bytes=40 * 1024 * 1024
        ),
        name="density_steps",
    )(density_map, offsets, velocities, weights, atom_cells, pair_tiles, halo_lists)


def solution(mesh):
    return jax.shard_map(
        per_device,
        mesh=mesh,
        in_specs=(
            P("dom", None, "slab"),
            P(None, "dom", "slab", None),
            P(None, "dom", "slab", None),
            P("dom", "slab", None),
            P(None, "dom", "slab", None),
            P("dom", "slab", None, None),
            P("dom", "slab", None, None),
        ),
        out_specs=(P(None, "dom", "slab", None), P(None, "dom", "slab", None)),
        check_vma=False,
    )
```

```python
import functools
import math

import jax
import jax.numpy as jnp
from jax import lax
from jax.experimental import pallas as pl
from jax.experimental.pallas import tpu as pltpu
from jax.sharding import PartitionSpec as P

REACH = 3
BLOCK = 256
BLOCKS = 2
TILES_PER = 3
STEPS = 3
ATOMS = 512
HALO = 128
DOMAINS = 64
SLABS = 8
X_CELLS = 64
Y_CELLS = 8
Z_CELLS = 128
ROWS = 16
BELOW = 4
Z_CHIPS, X_CHIPS, CORES = 8, 4, 2

FORCE_GAIN = 2.0
PAIR_GAIN = 0.1
PAIR_SOFT = 64.0
TIME_STEP = 0.25
SCALE = FORCE_GAIN * math.sqrt(float(X_CELLS * Y_CELLS * DOMAINS * Z_CELLS * SLABS * ATOMS * DOMAINS * SLABS))

MESH = pl.DeviceIdType.MESH
F32, BF16 = jnp.float32, jnp.bfloat16
BASE, U, V, CELL, WEIGHT, RECORD = 0, 3, 6, 9, 12, 16
LOWER, UPPER = 0, 1


def for_dom_peers(dom, do):
    z, x, core = dom // (X_CHIPS * CORES), dom // CORES % X_CHIPS, dom % CORES

    def along_x(dz):
        for dx in (2, 1, 3, 0):
            for dc in (1, 0):
                if isinstance(dz, int) and dz + dx + dc == 0:
                    continue
                peer = ((z + dz) % Z_CHIPS * X_CHIPS + (x + dx) % X_CHIPS) * CORES + (core + dc) % CORES
                do((dz * X_CHIPS + dx) * CORES + dc - 1, peer)

    def body(j, carry):
        along_x(Z_CHIPS // 2 + (1 - 2 * (j % 2)) * ((j + 1) // 2))
        return carry

    lax.fori_loop(0, Z_CHIPS - 1, body, 0)
    along_x(0)


def for_slab_peers(slab, do):
    for k in (4, 3, 5, 2, 6, 1, 7):
        do(k - 1, (slab + k) % SLABS)


def total_of(ref, count):
    sums = []
    for first in range(0, count, 16):
        sums.append(jnp.sum(ref[first : min(first + 16, count)], axis=0))
    return functools.reduce(jnp.add, sums)


def stencil(cell, moved, index):
    steps = index - cell
    spacing = steps - moved
    values = jnp.where(jnp.abs(steps) <= float(REACH), jnp.exp(-0.5 * spacing * spacing), 0.0)
    return values, values * spacing


def float_iota(shape, dim):
    return lax.broadcasted_iota(jnp.int32, shape, dim).astype(F32)


def kernel(
    map_hbm, offsets_hbm, velocities_hbm, weights_hbm, cells_hbm, tiles_hbm, lists_hbm,
    moved_out, speed_out, push_out,
    map_ref, offsets_ref, velocities_ref, weights_ref, cells_ref, tiles_ref, lists_ref, fetched,
    padded, map_send, map_recv, map_rows, windows, rho,
    records, record_recv, xf_pair, xf_pull, y_own, ys_own, y_near, z_near, zs_own,
    one_hot, rim_send, rim_recv, sources, state, pulls, ab, map_square,
    sums_send, dom_recv, slab_send, slab_recv,
    map_ssem, map_rsem, rec_ssem, rec_rsem, rim_ssem, rim_rsem, dom_ssem, dom_rsem, slab_ssem, slab_rsem,
):
    dom, slab = lax.axis_index("dom"), lax.axis_index("slab")
    lower, upper = (dom + DOMAINS - 1) % DOMAINS, (dom + 1) % DOMAINS
    before, after = (slab + SLABS - 1) % SLABS, (slab + 1) % SLABS

    fetches = [
        pltpu.make_async_copy(source, target, fetched.at[i])
        for i, (source, target) in enumerate((
            (map_hbm, map_ref), (offsets_hbm, offsets_ref), (velocities_hbm, velocities_ref), (weights_hbm, weights_ref),
            (cells_hbm, cells_ref), (tiles_hbm, tiles_ref), (lists_hbm, lists_ref),
        ))
    ]
    for fetch in fetches:
        fetch.start()

    barrier = pltpu.get_barrier_semaphore()

    def greet(k, carry):
        pl.semaphore_signal(barrier, inc=1, device_id=((dom + k) % DOMAINS, slab), device_id_type=MESH)
        return carry

    lax.fori_loop(1, DOMAINS, greet, 0)
    for k in range(1, SLABS):
        pl.semaphore_signal(barrier, inc=1, device_id=(dom, (slab + k) % SLABS), device_id_type=MESH)

    for fetch in fetches:
        fetch.wait()

    padded[0:8] = jnp.zeros((8, Z_CELLS), F32)
    padded[512:520] = jnp.zeros((8, Z_CELLS), F32)
    own_map = map_ref[0]
    padded[BELOW : BELOW + 512] = own_map
    square = own_map * own_map
    square = jnp.sum(jnp.sum(square.reshape(64, 8, Z_CELLS), axis=0), axis=0, keepdims=True)
    map_square[...] = square + pltpu.roll(square, 64, 1)

    def cut(t, carry):
        first = pl.multiple_of(t * Y_CELLS, Y_CELLS)
        map_send[t] = padded[pl.ds(first, ROWS)].astype(BF16)
        return carry

    lax.fori_loop(0, DOMAINS, cut, 0, unroll=8)
    map_recv[dom] = map_send[dom]

    weights = weights_ref[0]
    zero_row = jnp.zeros((1, ATOMS), F32)
    cell_rows = [cells_ref[i, 0].astype(F32) for i in range(3)]
    local_rows = [
        cell_rows[0],
        (cells_ref[1, 0] - dom * Y_CELLS).astype(F32),
        (cells_ref[2, 0] - slab * Z_CELLS).astype(F32),
    ]
    offset_rows = [offsets_ref[i, 0] for i in range(3)]
    fixed = local_rows + [weights] + [zero_row] * (RECORD - WEIGHT - 1)
    records[0] = jnp.concatenate(offset_rows + [zero_row] * 6 + fixed, axis=0)
    for i in range(3):
        state[i : i + 1] = zero_row
        state[3 + i : 4 + i] = velocities_ref[i, 0]
    ab[...] = jnp.zeros((8, ATOMS), F32)
    atom_index = lax.broadcasted_iota(jnp.int32, (ATOMS, HALO), 0)
    for entry in range(4):
        one_hot[:, entry * HALO : (entry + 1) * HALO] = jnp.where(
            atom_index == lists_ref[0, 0, entry : entry + 1, :], 1.0, 0.0
        ).astype(BF16)

    pl.semaphore_wait(barrier, DOMAINS - 1 + SLABS - 1)

    def record_copy(step, slot, peer):
        return pltpu.make_async_remote_copy(
            src_ref=records.at[step],
            dst_ref=record_recv.at[step, slot],
            send_sem=rec_ssem.at[step, slot],
            recv_sem=rec_rsem.at[step, slot],
            device_id=(peer, slab),
            device_id_type=MESH,
        )

    def send_records(step):
        record_copy(step, UPPER, lower).start()
        record_copy(step, LOWER, upper).start()

    send_records(0)

    def send_map(slot, peer):
        pltpu.make_async_remote_copy(
            src_ref=map_send.at[peer],
            dst_ref=map_recv.at[dom],
            send_sem=map_ssem,
            recv_sem=map_rsem,
            device_id=(peer, slab),
            device_id_type=MESH,
        ).start()

    for_dom_peers(dom, send_map)

    def step_body(step, carry):
        a_row, b_row = ab[0:1], ab[1:2]
        record_copy(step, LOWER, upper).wait_recv()
        record_copy(step, UPPER, lower).wait_recv()

        row = lax.broadcasted_iota(jnp.int32, (ROWS, ATOMS), 0)
        first_row = jnp.where(dom == 0, BELOW, 0)
        last_row = jnp.where(dom == DOMAINS - 1, BELOW + Y_CELLS, ROWS)
        in_grid = (row >= first_row) & (row < last_row)
        y_index = row.astype(F32) - float(BELOW)
        x_index = float_iota((X_CELLS, ATOMS), 0)
        z_index = float_iota((Z_CELLS, ATOMS), 0)
        own_moved = []
        for kind in range(3):
            record = records[step] if kind == 0 else record_recv[step, kind - 1]
            moved = [
                record[BASE + i : BASE + i + 1]
                + a_row * record[U + i : U + i + 1]
                + b_row * record[V + i : V + i + 1]
                for i in range(3)
            ]
            cell = [record[CELL + i : CELL + i + 1] for i in range(3)]
            heavy = record[WEIGHT : WEIGHT + 1]
            xv, xs = stencil(cell[0], moved[0], x_index)
            shift = (0.0, -float(Y_CELLS), float(Y_CELLS))[kind]
            yv, ys = stencil(cell[1] + shift, moved[1], y_index)
            zv, zs = stencil(cell[2], moved[2], z_index)
            xv = xv.astype(BF16)
            z_near[kind] = zv
            if kind == 0:
                xf_pair[0, :, 0:ATOMS] = xv
                xf_pair[1, :, 0:ATOMS] = xv
                xf_pull[:, 0:ATOMS] = xv
                xf_pull[:, ATOMS:] = xs.astype(BF16)
                zs_own[...] = zs
                y_own[...] = jnp.where(in_grid, heavy * yv, 0.0)
                ys_own[...] = heavy * ys
            else:
                xf_pair[kind - 1, :, ATOMS:] = xv
                there = (dom > 0) if kind == 1 else (dom < DOMAINS - 1)
                y_near[kind - 1] = jnp.where(in_grid & there, heavy * yv, 0.0)
            if kind == 0:
                own_moved = moved

        def spread_half(half, carry):
            def spread_row(i, carry):
                r = 1 + half * 7 + i
                cross = jnp.concatenate(
                    [
                        (y_own[pl.ds(r, 1)] * z_near[0]).astype(BF16),
                        (y_near[half, pl.ds(r, 1)] * z_near[half + 1]).astype(BF16),
                    ],
                    axis=1,
                )
                out = lax.dot_general(cross, xf_pair[half], (((1,), (1,)), ((), ())), preferred_element_type=F32)
                place = pl.ds(pl.multiple_of(r * Z_CELLS, Z_CELLS), Z_CELLS)
                rho[place] = out
                windows[1, place] = out.astype(BF16)
                return carry

            return lax.fori_loop(0, 7, spread_row, carry, unroll=7)

        lax.fori_loop(0, 2, spread_half, 0)

        @pl.when(step == 0)
        def _():
            everything = map_recv.at[pl.ds(0, DOMAINS - 1)]
            pltpu.make_async_copy(everything, everything, map_rsem).wait()
            map_rows[...] = map_recv[...].astype(F32).reshape(X_CELLS * ROWS, Z_CELLS)

            for r in range(ROWS):
                plane = map_rows[pl.ds(r, X_CELLS, stride=ROWS)]
                windows[0, r * Z_CELLS : (r + 1) * Z_CELLS] = plane.T.astype(BF16)

        def sum_row(r, carry):
            rr, rm = carry
            place = pl.ds(pl.multiple_of(r * Z_CELLS, Z_CELLS), Z_CELLS)
            here = rho[place].reshape(16, 8, X_CELLS)
            there = windows[0, place].astype(F32).reshape(16, 8, X_CELLS)
            return rr + jnp.sum(here * here, axis=0), rm + jnp.sum(here * there, axis=0)

        nothing = jnp.zeros((8, X_CELLS), F32)
        rr, rm = lax.fori_loop(BELOW, BELOW + Y_CELLS, sum_row, (nothing, nothing))
        both = jnp.concatenate(
            [jnp.sum(rr, axis=0, keepdims=True), jnp.sum(rm, axis=0, keepdims=True)], axis=1
        )
        both = both + pltpu.roll(both, 96, 1)
        lane = lax.broadcasted_iota(jnp.int32, (1, 128), 1)
        sums = jnp.where(lane < 64, both, map_square[...])
        sums_send[step] = jnp.where((lane >= 32) & (lane < 64), pltpu.roll(both, 96, 1), sums)

        def dom_copy(slot, peer):
            pltpu.make_async_remote_copy(
                src_ref=sums_send.at[step],
                dst_ref=dom_recv.at[step, slot],
                send_sem=dom_ssem.at[step],
                recv_sem=dom_rsem.at[step],
                device_id=(peer, slab),
                device_id_type=MESH,
            ).start()

        for_dom_peers(dom, dom_copy)

        positions = jnp.concatenate([cell_rows[i] + own_moved[i] for i in range(3)] + [weights] + [zero_row] * 4, axis=0)
        high = positions.astype(BF16).astype(F32)
        middle = (positions - high).astype(BF16).astype(F32)
        low = positions - high - middle
        split = jnp.concatenate([high, middle, low, jnp.zeros((8, ATOMS), F32)], axis=0).astype(BF16)
        listed = jnp.dot(split, one_hot[...], preferred_element_type=F32)
        listed = listed[0:8] + listed[8:16] + listed[16:24]

        def rim_copy(entry):
            slot, place = (
                (1, (lower, slab)), (0, (upper, slab)), (3, (dom, before)), (2, (dom, after)),
            )[entry]
            return pltpu.make_async_remote_copy(
                src_ref=rim_send.at[step, entry],
                dst_ref=rim_recv.at[step, slot],
                send_sem=rim_ssem.at[step, entry],
                recv_sem=rim_rsem.at[step, slot],
                device_id=place,
                device_id_type=MESH,
            )

        for entry in range(4):
            rim_send[step, entry] = listed[:, entry * HALO : (entry + 1) * HALO]
            rim_copy(entry).start()

        def pull(which, carry):
            def pull_row(r, sums):
                place = pl.ds(pl.multiple_of(r * Z_CELLS, Z_CELLS), Z_CELLS)
                window = windows[which, place]
                yv, ys = y_own[pl.ds(r, 1)], ys_own[pl.ds(r, 1)]
                out = []
                for half in range(2):
                    at = slice(half * 256, (half + 1) * 256)
                    plain = jnp.dot(window, xf_pull[:, half * 256 : (half + 1) * 256], preferred_element_type=F32)
                    sloped = jnp.dot(window, xf_pull[:, ATOMS + half * 256 : ATOMS + (half + 1) * 256], preferred_element_type=F32)
                    zv, zs = z_near[0, :, at], zs_own[:, at]

                    def over_z(product):
                        return jnp.sum(product.reshape(16, 8, 256), axis=0)

                    out.append(sums[half * 3] + over_z(sloped * zv) * yv[:, at])
                    out.append(sums[half * 3 + 1] + over_z(plain * zv) * ys[:, at])
                    out.append(sums[half * 3 + 2] + over_z(plain * zs) * yv[:, at])
                return tuple(out)

            sums = lax.fori_loop(1, ROWS - 1, pull_row, (jnp.zeros((8, 256), F32),) * 6, unroll=7)
            for half in range(2):
                rows = [jnp.sum(sums[half * 3 + i], axis=0, keepdims=True) for i in range(3)]
                pulls[which, :, half * 256 : (half + 1) * 256] = jnp.concatenate(rows + [jnp.zeros((5, 256), F32)], axis=0)
            return carry

        lax.fori_loop(0, 2, pull, 0)

        rims = []
        for slot in range(4):
            rim_copy((1, 0, 3, 2)[slot]).wait_recv()
            there = ((dom > 0), (dom < DOMAINS - 1), (slab > 0), (slab < SLABS - 1))[slot]
            keep = (lax.broadcasted_iota(jnp.int32, (8, HALO), 0) != 3) | there
            rims.append(jnp.where(keep, rim_recv[step, slot], 0.0))
        blocks = [positions[:, 0:BLOCK], positions[:, BLOCK:]]
        blocks += [jnp.concatenate(rims[0:2], axis=1), jnp.concatenate(rims[2:4], axis=1)]
        for block in range(BLOCKS):
            for j in range(TILES_PER):
                listed_block = blocks[block]
                if j > 0:
                    source = jnp.broadcast_to(tiles_ref[0, 0, block : block + 1, j : j + 1], (8, BLOCK))
                    listed_block = blocks[3]
                    for t in range(3):
                        listed_block = jnp.where(source == t, blocks[t], listed_block)
                sources[block, j * BLOCK : (j + 1) * BLOCK] = listed_block.T
        pair_rows = []
        for block in range(BLOCKS):
            at = slice(block * BLOCK, (block + 1) * BLOCK)
            near = [positions[i : i + 1, at] for i in range(3)]

            def chunk(c, total, block=block, near=near):
                far = sources[block, pl.ds(pl.multiple_of(c * 32, 32), 32)]
                between = [near[i] - far[:, i : i + 1] for i in range(3)]
                squared = between[0] * between[0] + between[1] * between[1] + between[2] * between[2] + PAIR_SOFT
                inverse = lax.rsqrt(squared)
                falloff = far[:, 3:4] * (inverse * inverse * inverse)
                return tuple(
                    total[i] + jnp.sum((between[i] * falloff).reshape(4, 8, BLOCK), axis=0) for i in range(3)
                )

            total = lax.fori_loop(0, TILES_PER * BLOCK // 32, chunk, (jnp.zeros((8, BLOCK), F32),) * 3, unroll=12)
            pair_rows.append([jnp.sum(t, axis=0, keepdims=True) for t in total])

        gain = TIME_STEP * TIME_STEP * SCALE
        u_rows, v_rows, base_rows = [], [], []
        for i in range(3):
            pair = jnp.concatenate([pair_rows[block][i] for block in range(BLOCKS)], axis=1)
            speed = state[3 + i : 4 + i] + TIME_STEP * (PAIR_GAIN * weights * pair)
            state[3 + i : 4 + i] = speed
            base_rows.append(own_moved[i] + TIME_STEP * speed)
            u_rows.append(gain * pulls[0, i : i + 1])
            v_rows.append(-gain * pulls[1, i : i + 1])
        record = jnp.concatenate(base_rows + u_rows + v_rows + fixed, axis=0)

        @pl.when(step < STEPS - 1)
        def _():
            records[step + 1] = record
            send_records(step + 1)

        pltpu.make_async_copy(dom_recv.at[step], dom_recv.at[step], dom_rsem.at[step]).wait()
        slab_send[step] = sums_send[step] + total_of(dom_recv.at[step], DOMAINS - 1)

        def slab_copy(slot, peer):
            pltpu.make_async_remote_copy(
                src_ref=slab_send.at[step],
                dst_ref=slab_recv.at[step, slot],
                send_sem=slab_ssem.at[step],
                recv_sem=slab_rsem.at[step],
                device_id=(dom, peer),
                device_id_type=MESH,
            ).start()

        for_slab_peers(slab, slab_copy)
        pltpu.make_async_copy(slab_recv.at[step], slab_recv.at[step], slab_rsem.at[step]).wait()
        sums = slab_send[step] + total_of(slab_recv.at[step], SLABS - 1)
        srr = jnp.sum(jnp.where(lane < 32, sums, 0.0), axis=1, keepdims=True)
        srm = jnp.sum(jnp.where((lane >= 32) & (lane < 64), sums, 0.0), axis=1, keepdims=True)
        smm = jnp.sum(jnp.where(lane >= 64, sums, 0.0), axis=1, keepdims=True)
        norm = jnp.sqrt(srr * smm)
        a = 1.0 / norm
        b = srm / (norm * srr)
        ab[0:1] = jnp.broadcast_to(a, (1, ATOMS))
        ab[1:2] = jnp.broadcast_to(b, (1, ATOMS))
        for i in range(3):
            push = (a * u_rows[i] + b * v_rows[i]) * (1.0 / TIME_STEP)
            speed_out[i, 0] = state[3 + i : 4 + i]
            push_out[i, 0] = push
            moved_out[i, 0] = state[i : i + 1]
            speed = state[3 + i : 4 + i] + push
            state[3 + i : 4 + i] = speed
            state[i : i + 1] = state[i : i + 1] + TIME_STEP * speed
        return carry

    lax.fori_loop(0, STEPS, step_body, 0)
    everything = map_send.at[pl.ds(0, DOMAINS - 1)]
    pltpu.make_async_copy(everything, everything, map_ssem).wait()

    def drain(step, carry):
        record_copy(step, UPPER, lower).wait_send()
        record_copy(step, LOWER, upper).wait_send()
        for entry in range(4):
            pltpu.make_async_copy(rim_send.at[step, entry], rim_send.at[step, entry], rim_ssem.at[step, entry]).wait()
        pltpu.make_async_copy(dom_recv.at[step], dom_recv.at[step], dom_ssem.at[step]).wait()
        pltpu.make_async_copy(slab_recv.at[step], slab_recv.at[step], slab_ssem.at[step]).wait()
        return carry

    lax.fori_loop(0, STEPS, drain, 0)


def per_device(density_map, offsets, velocities, weights, atom_cells, pair_tiles, halo_lists):
    vmem = pl.BlockSpec(memory_space=pltpu.VMEM)
    hbm = pl.BlockSpec(memory_space=pltpu.HBM)
    arguments = (density_map, offsets, velocities, weights, atom_cells, pair_tiles, halo_lists)
    out = jax.ShapeDtypeStruct(offsets.shape, F32)
    dma = pltpu.SemaphoreType.DMA
    scratch = [
        *[pltpu.VMEM(argument.shape, argument.dtype) for argument in arguments],
        dma((len(arguments),)),
        pltpu.VMEM((520, Z_CELLS), F32),
        pltpu.VMEM((DOMAINS, ROWS, Z_CELLS), BF16),
        pltpu.VMEM((X_CELLS, ROWS, Z_CELLS), BF16),
        pltpu.VMEM((X_CELLS * ROWS, Z_CELLS), F32),
        pltpu.VMEM((2, ROWS * Z_CELLS, X_CELLS), BF16),
        pltpu.VMEM((ROWS * Z_CELLS, X_CELLS), F32),
        pltpu.VMEM((STEPS, RECORD, ATOMS), F32),
        pltpu.VMEM((STEPS, 2, RECORD, ATOMS), F32),
        pltpu.VMEM((2, X_CELLS, 2 * ATOMS), BF16),
        pltpu.VMEM((X_CELLS, 2 * ATOMS), BF16),
        pltpu.VMEM((ROWS, ATOMS), F32),
        pltpu.VMEM((ROWS, ATOMS), F32),
        pltpu.VMEM((2, ROWS, ATOMS), F32),
        pltpu.VMEM((3, Z_CELLS, ATOMS), F32),
        pltpu.VMEM((Z_CELLS, ATOMS), F32),
        pltpu.VMEM((ATOMS, 4 * HALO), BF16),
        pltpu.VMEM((STEPS, 4, 8, HALO), F32),
        pltpu.VMEM((STEPS, 4, 8, HALO), F32),
        pltpu.VMEM((BLOCKS, TILES_PER * BLOCK, 8), F32),
        pltpu.VMEM((8, ATOMS), F32),
        pltpu.VMEM((2, 8, ATOMS), F32),
        pltpu.VMEM((8, ATOMS), F32),
        pltpu.VMEM((1, 128), F32),
        pltpu.VMEM((STEPS, 1, 128), F32),
        pltpu.VMEM((STEPS, DOMAINS - 1, 1, 128), F32),
        pltpu.VMEM((STEPS, 1, 128), F32),
        pltpu.VMEM((STEPS, SLABS - 1, 1, 128), F32),
        dma, dma,
        dma((STEPS, 2)), dma((STEPS, 2)),
        dma((STEPS, 4)), dma((STEPS, 4)),
        dma((STEPS,)), dma((STEPS,)),
        dma((STEPS,)), dma((STEPS,)),
    ]
    moved, speed, push = pl.pallas_call(
        kernel,
        out_shape=(out, out, out),
        in_specs=[hbm] * len(arguments),
        out_specs=(vmem, vmem, vmem),
        scratch_shapes=scratch,
        compiler_params=pltpu.CompilerParams(
            collective_id=0, has_side_effects=True, vmem_limit_bytes=56 * 1024 * 1024
        ),
        name="density_steps",
    )(*arguments)
    speed = speed + push
    return moved + TIME_STEP * speed, speed


def solution(mesh):
    return jax.shard_map(
        per_device,
        mesh=mesh,
        in_specs=(
            P("dom", None, "slab"),
            P(None, "dom", "slab", None),
            P(None, "dom", "slab", None),
            P("dom", "slab", None),
            P(None, "dom", "slab", None),
            P("dom", "slab", None, None),
            P("dom", "slab", None, None),
        ),
        out_specs=(P(None, "dom", "slab", None), P(None, "dom", "slab", None)),
        check_vma=False,
    )
```

```python
import functools
import math

import jax
import jax.numpy as jnp
from jax import lax
from jax.experimental import pallas as pl
from jax.experimental.pallas import tpu as pltpu
from jax.sharding import PartitionSpec as P

REACH = 3
BLOCK = 256
BLOCKS = 2
TILES_PER = 3
STEPS = 3
ATOMS = 512
HALO = 128
DOMAINS = 64
SLABS = 8
X_CELLS = 64
Y_CELLS = 8
Z_CELLS = 128
ROWS = 16
BELOW = 4
Z_CHIPS, X_CHIPS, CORES = 8, 4, 2

FORCE_GAIN = 2.0
PAIR_GAIN = 0.1
PAIR_SOFT = 64.0
TIME_STEP = 0.25
SCALE = FORCE_GAIN * math.sqrt(float(X_CELLS * Y_CELLS * DOMAINS * Z_CELLS * SLABS * ATOMS * DOMAINS * SLABS))

MESH = pl.DeviceIdType.MESH
F32, BF16 = jnp.float32, jnp.bfloat16
BASE, U, V, CELL, WEIGHT, RECORD = 0, 3, 6, 9, 12, 16
LOWER, UPPER = 0, 1


def for_dom_peers(dom, do):
    z, x, core = dom // (X_CHIPS * CORES), dom // CORES % X_CHIPS, dom % CORES

    def along_x(dz):
        for dx in (2, 1, 3, 0):
            for dc in (1, 0):
                if isinstance(dz, int) and dz + dx + dc == 0:
                    continue
                peer = ((z + dz) % Z_CHIPS * X_CHIPS + (x + dx) % X_CHIPS) * CORES + (core + dc) % CORES
                do((dz * X_CHIPS + dx) * CORES + dc - 1, peer)

    def body(j, carry):
        along_x(Z_CHIPS // 2 + (1 - 2 * (j % 2)) * ((j + 1) // 2))
        return carry

    lax.fori_loop(0, Z_CHIPS - 1, body, 0)
    along_x(0)


def for_slab_peers(slab, do):
    for k in (4, 3, 5, 2, 6, 1, 7):
        do(k - 1, (slab + k) % SLABS)


def total_of(ref, count):
    sums = []
    for first in range(0, count, 16):
        sums.append(jnp.sum(ref[first : min(first + 16, count)], axis=0))
    return functools.reduce(jnp.add, sums)


def stencil(cell, moved, index):
    steps = index - cell
    spacing = steps - moved
    values = jnp.where(jnp.abs(steps) <= float(REACH), jnp.exp(-0.5 * spacing * spacing), 0.0)
    return values, values * spacing


def float_iota(shape, dim):
    return lax.broadcasted_iota(jnp.int32, shape, dim).astype(F32)


def kernel(
    map_hbm, offsets_hbm, velocities_hbm, weights_hbm, cells_hbm, tiles_hbm, lists_hbm,
    moved_out, speed_out, push_out,
    map_ref, offsets_ref, velocities_ref, weights_ref, cells_ref, tiles_ref, lists_ref, fetched,
    padded, map_send, map_recv, map_rows, windows, rho,
    records, record_recv, xf_pair, xf_pull, y_own, ys_own, y_near, z_near, zs_own,
    one_hot, rim_send, rim_recv, sources, state, pulls, ab, map_square,
    sums_send, dom_recv, slab_send, slab_recv,
    map_ssem, map_rsem, rec_ssem, rec_rsem, rim_ssem, rim_rsem, dom_ssem, dom_rsem, slab_ssem, slab_rsem,
):
    dom, slab = lax.axis_index("dom"), lax.axis_index("slab")
    lower, upper = (dom + DOMAINS - 1) % DOMAINS, (dom + 1) % DOMAINS
    before, after = (slab + SLABS - 1) % SLABS, (slab + 1) % SLABS

    fetches = [
        pltpu.make_async_copy(source, target, fetched.at[i])
        for i, (source, target) in enumerate((
            (map_hbm, map_ref), (offsets_hbm, offsets_ref), (velocities_hbm, velocities_ref), (weights_hbm, weights_ref),
            (cells_hbm, cells_ref), (tiles_hbm, tiles_ref), (lists_hbm, lists_ref),
        ))
    ]
    for fetch in fetches:
        fetch.start()

    barrier = pltpu.get_barrier_semaphore()

    def greet(slot, peer):
        pl.semaphore_signal(barrier, inc=1, device_id=(peer, slab), device_id_type=MESH)

    for_dom_peers(dom, greet)
    for k in range(1, SLABS):
        pl.semaphore_signal(barrier, inc=1, device_id=(dom, (slab + k) % SLABS), device_id_type=MESH)

    for fetch in fetches:
        fetch.wait()

    padded[0:8] = jnp.zeros((8, Z_CELLS), F32)
    padded[512:520] = jnp.zeros((8, Z_CELLS), F32)
    own_map = map_ref[0]
    padded[BELOW : BELOW + 512] = own_map
    square = own_map * own_map
    square = jnp.sum(jnp.sum(square.reshape(64, 8, Z_CELLS), axis=0), axis=0, keepdims=True)
    map_square[...] = square + pltpu.roll(square, 64, 1)

    def cut(t, carry):
        first = pl.multiple_of(t * Y_CELLS, Y_CELLS)
        map_send[t] = padded[pl.ds(first, ROWS)].astype(BF16)
        return carry

    lax.fori_loop(0, DOMAINS, cut, 0, unroll=8)
    map_recv[dom] = map_send[dom]

    weights = weights_ref[0]
    zero_row = jnp.zeros((1, ATOMS), F32)
    cell_rows = [cells_ref[i, 0].astype(F32) for i in range(3)]
    local_rows = [
        cell_rows[0],
        (cells_ref[1, 0] - dom * Y_CELLS).astype(F32),
        (cells_ref[2, 0] - slab * Z_CELLS).astype(F32),
    ]
    offset_rows = [offsets_ref[i, 0] for i in range(3)]
    fixed = local_rows + [weights] + [zero_row] * (RECORD - WEIGHT - 1)
    records[0] = jnp.concatenate(offset_rows + [zero_row] * 6 + fixed, axis=0)
    for i in range(3):
        state[i : i + 1] = zero_row
        state[3 + i : 4 + i] = velocities_ref[i, 0]
    ab[...] = jnp.zeros((8, ATOMS), F32)
    atom_index = lax.broadcasted_iota(jnp.int32, (ATOMS, HALO), 0)
    for entry in range(4):
        one_hot[:, entry * HALO : (entry + 1) * HALO] = jnp.where(
            atom_index == lists_ref[0, 0, entry : entry + 1, :], 1.0, 0.0
        ).astype(BF16)

    pl.semaphore_wait(barrier, DOMAINS - 1 + SLABS - 1)

    def record_copy(step, slot, peer):
        return pltpu.make_async_remote_copy(
            src_ref=records.at[step],
            dst_ref=record_recv.at[step, slot],
            send_sem=rec_ssem.at[step, slot],
            recv_sem=rec_rsem.at[step, slot],
            device_id=(peer, slab),
            device_id_type=MESH,
        )

    def send_records(step):
        record_copy(step, UPPER, lower).start()
        record_copy(step, LOWER, upper).start()

    send_records(0)

    def send_map(slot, peer):
        pltpu.make_async_remote_copy(
            src_ref=map_send.at[peer],
            dst_ref=map_recv.at[dom],
            send_sem=map_ssem,
            recv_sem=map_rsem,
            device_id=(peer, slab),
            device_id_type=MESH,
        ).start()

    for_dom_peers(dom, send_map)

    def step_body(step, carry):
        a_row, b_row = ab[0:1], ab[1:2]
        record_copy(step, LOWER, upper).wait_recv()
        record_copy(step, UPPER, lower).wait_recv()

        row = lax.broadcasted_iota(jnp.int32, (ROWS, ATOMS), 0)
        first_row = jnp.where(dom == 0, BELOW, 0)
        last_row = jnp.where(dom == DOMAINS - 1, BELOW + Y_CELLS, ROWS)
        in_grid = (row >= first_row) & (row < last_row)
        y_index = row.astype(F32) - float(BELOW)
        x_index = float_iota((X_CELLS, ATOMS), 0)
        z_index = float_iota((Z_CELLS, ATOMS), 0)
        own_moved = []
        for kind in range(3):
            record = records[step] if kind == 0 else record_recv[step, kind - 1]
            moved = [
                record[BASE + i : BASE + i + 1]
                + a_row * record[U + i : U + i + 1]
                + b_row * record[V + i : V + i + 1]
                for i in range(3)
            ]
            cell = [record[CELL + i : CELL + i + 1] for i in range(3)]
            heavy = record[WEIGHT : WEIGHT + 1]
            xv, xs = stencil(cell[0], moved[0], x_index)
            shift = (0.0, -float(Y_CELLS), float(Y_CELLS))[kind]
            yv, ys = stencil(cell[1] + shift, moved[1], y_index)
            zv, zs = stencil(cell[2], moved[2], z_index)
            xv = xv.astype(BF16)
            z_near[kind] = zv
            if kind == 0:
                xf_pair[0, :, 0:ATOMS] = xv
                xf_pair[1, :, 0:ATOMS] = xv
                xf_pull[:, 0:ATOMS] = xv
                xf_pull[:, ATOMS:] = xs.astype(BF16)
                zs_own[...] = zs
                y_own[...] = jnp.where(in_grid, heavy * yv, 0.0)
                ys_own[...] = heavy * ys
            else:
                xf_pair[kind - 1, :, ATOMS:] = xv
                there = (dom > 0) if kind == 1 else (dom < DOMAINS - 1)
                y_near[kind - 1] = jnp.where(in_grid & there, heavy * yv, 0.0)
            if kind == 0:
                own_moved = moved

        positions = jnp.concatenate([cell_rows[i] + own_moved[i] for i in range(3)] + [weights] + [zero_row] * 4, axis=0)
        high = positions.astype(BF16).astype(F32)
        middle = (positions - high).astype(BF16).astype(F32)
        low = positions - high - middle
        split = jnp.concatenate([high, middle, low, jnp.zeros((8, ATOMS), F32)], axis=0).astype(BF16)
        listed = jnp.dot(split, one_hot[...], preferred_element_type=F32)
        listed = listed[0:8] + listed[8:16] + listed[16:24]

        def rim_copy(entry):
            slot, place = (
                (1, (lower, slab)), (0, (upper, slab)), (3, (dom, before)), (2, (dom, after)),
            )[entry]
            return pltpu.make_async_remote_copy(
                src_ref=rim_send.at[step, entry],
                dst_ref=rim_recv.at[step, slot],
                send_sem=rim_ssem.at[step, entry],
                recv_sem=rim_rsem.at[step, slot],
                device_id=place,
                device_id_type=MESH,
            )

        for entry in range(4):
            rim_send[step, entry] = listed[:, entry * HALO : (entry + 1) * HALO]
            rim_copy(entry).start()

        def spread(first, rows, apart):
            def spread_half(half, carry):
                def spread_row(i, carry):
                    r = first + half * apart + i
                    cross = jnp.concatenate(
                        [
                            (y_own[pl.ds(r, 1)] * z_near[0]).astype(BF16),
                            (y_near[half, pl.ds(r, 1)] * z_near[half + 1]).astype(BF16),
                        ],
                        axis=1,
                    )
                    out = lax.dot_general(cross, xf_pair[half], (((1,), (1,)), ((), ())), preferred_element_type=F32)
                    place = pl.ds(pl.multiple_of(r * Z_CELLS, Z_CELLS), Z_CELLS)
                    rho[place] = out
                    windows[1, place] = out.astype(BF16)
                    return carry

                return lax.fori_loop(0, rows, spread_row, carry, unroll=rows)

            lax.fori_loop(0, 2, spread_half, 0)

        spread(BELOW, Y_CELLS // 2, Y_CELLS // 2)

        @pl.when(step == 0)
        def _():
            everything = map_recv.at[pl.ds(0, DOMAINS - 1)]
            pltpu.make_async_copy(everything, everything, map_rsem).wait()
            map_rows[...] = map_recv[...].astype(F32).reshape(X_CELLS * ROWS, Z_CELLS)

            for r in range(ROWS):
                plane = map_rows[pl.ds(r, X_CELLS, stride=ROWS)]
                windows[0, r * Z_CELLS : (r + 1) * Z_CELLS] = plane.T.astype(BF16)

        def sum_row(r, carry):
            rr, rm = carry
            place = pl.ds(pl.multiple_of(r * Z_CELLS, Z_CELLS), Z_CELLS)
            here = rho[place].reshape(16, 8, X_CELLS)
            there = windows[0, place].astype(F32).reshape(16, 8, X_CELLS)
            return rr + jnp.sum(here * here, axis=0), rm + jnp.sum(here * there, axis=0)

        nothing = jnp.zeros((8, X_CELLS), F32)
        rr, rm = lax.fori_loop(BELOW, BELOW + Y_CELLS, sum_row, (nothing, nothing))
        both = jnp.concatenate(
            [jnp.sum(rr, axis=0, keepdims=True), jnp.sum(rm, axis=0, keepdims=True)], axis=1
        )
        both = both + pltpu.roll(both, 96, 1)
        lane = lax.broadcasted_iota(jnp.int32, (1, 128), 1)
        sums = jnp.where(lane < 64, both, map_square[...])
        sums_send[step] = jnp.where((lane >= 32) & (lane < 64), pltpu.roll(both, 96, 1), sums)

        def dom_copy(slot, peer):
            pltpu.make_async_remote_copy(
                src_ref=sums_send.at[step],
                dst_ref=dom_recv.at[step, slot],
                send_sem=dom_ssem.at[step],
                recv_sem=dom_rsem.at[step],
                device_id=(peer, slab),
                device_id_type=MESH,
            ).start()

        for_dom_peers(dom, dom_copy)
        spread(1, REACH, BELOW + Y_CELLS - 1)

        def pull(which, carry):
            def pull_row(r, sums):
                place = pl.ds(pl.multiple_of(r * Z_CELLS, Z_CELLS), Z_CELLS)
                window = windows[which, place]
                yv, ys = y_own[pl.ds(r, 1)], ys_own[pl.ds(r, 1)]
                out = []
                for half in range(2):
                    at = slice(half * 256, (half + 1) * 256)
                    plain = jnp.dot(window, xf_pull[:, half * 256 : (half + 1) * 256], preferred_element_type=F32)
                    sloped = jnp.dot(window, xf_pull[:, ATOMS + half * 256 : ATOMS + (half + 1) * 256], preferred_element_type=F32)
                    zv, zs = z_near[0, :, at], zs_own[:, at]

                    def over_z(product):
                        return jnp.sum(product.reshape(16, 8, 256), axis=0)

                    out.append(sums[half * 3] + over_z(sloped * zv) * yv[:, at])
                    out.append(sums[half * 3 + 1] + over_z(plain * zv) * ys[:, at])
                    out.append(sums[half * 3 + 2] + over_z(plain * zs) * yv[:, at])
                return tuple(out)

            sums = lax.fori_loop(1, ROWS - 1, pull_row, (jnp.zeros((8, 256), F32),) * 6, unroll=7)
            for half in range(2):
                rows = [jnp.sum(sums[half * 3 + i], axis=0, keepdims=True) for i in range(3)]
                pulls[which, :, half * 256 : (half + 1) * 256] = jnp.concatenate(rows + [jnp.zeros((5, 256), F32)], axis=0)
            return carry

        lax.fori_loop(0, 2, pull, 0)

        rims = []
        for slot in range(4):
            rim_copy((1, 0, 3, 2)[slot]).wait_recv()
            there = ((dom > 0), (dom < DOMAINS - 1), (slab > 0), (slab < SLABS - 1))[slot]
            keep = (lax.broadcasted_iota(jnp.int32, (8, HALO), 0) != 3) | there
            rims.append(jnp.where(keep, rim_recv[step, slot], 0.0))
        blocks = [positions[:, 0:BLOCK], positions[:, BLOCK:]]
        blocks += [jnp.concatenate(rims[0:2], axis=1), jnp.concatenate(rims[2:4], axis=1)]
        for block in range(BLOCKS):
            for j in range(TILES_PER):
                listed_block = blocks[block]
                if j > 0:
                    source = jnp.broadcast_to(tiles_ref[0, 0, block : block + 1, j : j + 1], (8, BLOCK))
                    listed_block = blocks[3]
                    for t in range(3):
                        listed_block = jnp.where(source == t, blocks[t], listed_block)
                sources[block, j * BLOCK : (j + 1) * BLOCK] = listed_block.T
        pair_rows = []
        for block in range(BLOCKS):
            at = slice(block * BLOCK, (block + 1) * BLOCK)
            near = [positions[i : i + 1, at] for i in range(3)]

            def chunk(c, total, block=block, near=near):
                far = sources[block, pl.ds(pl.multiple_of(c * 32, 32), 32)]
                between = [near[i] - far[:, i : i + 1] for i in range(3)]
                squared = between[0] * between[0] + between[1] * between[1] + between[2] * between[2] + PAIR_SOFT
                inverse = lax.rsqrt(squared)
                falloff = far[:, 3:4] * (inverse * inverse * inverse)
                return tuple(
                    total[i] + jnp.sum((between[i] * falloff).reshape(4, 8, BLOCK), axis=0) for i in range(3)
                )

            total = lax.fori_loop(0, TILES_PER * BLOCK // 32, chunk, (jnp.zeros((8, BLOCK), F32),) * 3, unroll=12)
            pair_rows.append([jnp.sum(t, axis=0, keepdims=True) for t in total])

        gain = TIME_STEP * TIME_STEP * SCALE
        u_rows, v_rows, base_rows = [], [], []
        for i in range(3):
            pair = jnp.concatenate([pair_rows[block][i] for block in range(BLOCKS)], axis=1)
            speed = state[3 + i : 4 + i] + TIME_STEP * (PAIR_GAIN * weights * pair)
            state[3 + i : 4 + i] = speed
            base_rows.append(own_moved[i] + TIME_STEP * speed)
            u_rows.append(gain * pulls[0, i : i + 1])
            v_rows.append(-gain * pulls[1, i : i + 1])
        record = jnp.concatenate(base_rows + u_rows + v_rows + fixed, axis=0)

        @pl.when(step < STEPS - 1)
        def _():
            records[step + 1] = record
            send_records(step + 1)

        pltpu.make_async_copy(dom_recv.at[step], dom_recv.at[step], dom_rsem.at[step]).wait()
        slab_send[step] = sums_send[step] + total_of(dom_recv.at[step], DOMAINS - 1)

        def slab_copy(slot, peer):
            pltpu.make_async_remote_copy(
                src_ref=slab_send.at[step],
                dst_ref=slab_recv.at[step, slot],
                send_sem=slab_ssem.at[step],
                recv_sem=slab_rsem.at[step],
                device_id=(dom, peer),
                device_id_type=MESH,
            ).start()

        for_slab_peers(slab, slab_copy)
        pltpu.make_async_copy(slab_recv.at[step], slab_recv.at[step], slab_rsem.at[step]).wait()
        sums = slab_send[step] + total_of(slab_recv.at[step], SLABS - 1)
        srr = jnp.sum(jnp.where(lane < 32, sums, 0.0), axis=1, keepdims=True)
        srm = jnp.sum(jnp.where((lane >= 32) & (lane < 64), sums, 0.0), axis=1, keepdims=True)
        smm = jnp.sum(jnp.where(lane >= 64, sums, 0.0), axis=1, keepdims=True)
        norm = jnp.sqrt(srr * smm)
        a = 1.0 / norm
        b = srm / (norm * srr)
        ab[0:1] = jnp.broadcast_to(a, (1, ATOMS))
        ab[1:2] = jnp.broadcast_to(b, (1, ATOMS))
        for i in range(3):
            push = (a * u_rows[i] + b * v_rows[i]) * (1.0 / TIME_STEP)
            speed_out[i, 0] = state[3 + i : 4 + i]
            push_out[i, 0] = push
            moved_out[i, 0] = state[i : i + 1]
            speed = state[3 + i : 4 + i] + push
            state[3 + i : 4 + i] = speed
            state[i : i + 1] = state[i : i + 1] + TIME_STEP * speed
        return carry

    lax.fori_loop(0, STEPS, step_body, 0)
    everything = map_send.at[pl.ds(0, DOMAINS - 1)]
    pltpu.make_async_copy(everything, everything, map_ssem).wait()

    def drain(step, carry):
        record_copy(step, UPPER, lower).wait_send()
        record_copy(step, LOWER, upper).wait_send()
        for entry in range(4):
            pltpu.make_async_copy(rim_send.at[step, entry], rim_send.at[step, entry], rim_ssem.at[step, entry]).wait()
        pltpu.make_async_copy(dom_recv.at[step], dom_recv.at[step], dom_ssem.at[step]).wait()
        pltpu.make_async_copy(slab_recv.at[step], slab_recv.at[step], slab_ssem.at[step]).wait()
        return carry

    lax.fori_loop(0, STEPS, drain, 0)


def per_device(density_map, offsets, velocities, weights, atom_cells, pair_tiles, halo_lists):
    vmem = pl.BlockSpec(memory_space=pltpu.VMEM)
    hbm = pl.BlockSpec(memory_space=pltpu.HBM)
    arguments = (density_map, offsets, velocities, weights, atom_cells, pair_tiles, halo_lists)
    out = jax.ShapeDtypeStruct(offsets.shape, F32)
    dma = pltpu.SemaphoreType.DMA
    scratch = [
        *[pltpu.VMEM(argument.shape, argument.dtype) for argument in arguments],
        dma((len(arguments),)),
        pltpu.VMEM((520, Z_CELLS), F32),
        pltpu.VMEM((DOMAINS, ROWS, Z_CELLS), BF16),
        pltpu.VMEM((X_CELLS, ROWS, Z_CELLS), BF16),
        pltpu.VMEM((X_CELLS * ROWS, Z_CELLS), F32),
        pltpu.VMEM((2, ROWS * Z_CELLS, X_CELLS), BF16),
        pltpu.VMEM((ROWS * Z_CELLS, X_CELLS), F32),
        pltpu.VMEM((STEPS, RECORD, ATOMS), F32),
        pltpu.VMEM((STEPS, 2, RECORD, ATOMS), F32),
        pltpu.VMEM((2, X_CELLS, 2 * ATOMS), BF16),
        pltpu.VMEM((X_CELLS, 2 * ATOMS), BF16),
        pltpu.VMEM((ROWS, ATOMS), F32),
        pltpu.VMEM((ROWS, ATOMS), F32),
        pltpu.VMEM((2, ROWS, ATOMS), F32),
        pltpu.VMEM((3, Z_CELLS, ATOMS), F32),
        pltpu.VMEM((Z_CELLS, ATOMS), F32),
        pltpu.VMEM((ATOMS, 4 * HALO), BF16),
        pltpu.VMEM((STEPS, 4, 8, HALO), F32),
        pltpu.VMEM((STEPS, 4, 8, HALO), F32),
        pltpu.VMEM((BLOCKS, TILES_PER * BLOCK, 8), F32),
        pltpu.VMEM((8, ATOMS), F32),
        pltpu.VMEM((2, 8, ATOMS), F32),
        pltpu.VMEM((8, ATOMS), F32),
        pltpu.VMEM((1, 128), F32),
        pltpu.VMEM((STEPS, 1, 128), F32),
        pltpu.VMEM((STEPS, DOMAINS - 1, 1, 128), F32),
        pltpu.VMEM((STEPS, 1, 128), F32),
        pltpu.VMEM((STEPS, SLABS - 1, 1, 128), F32),
        dma, dma,
        dma((STEPS, 2)), dma((STEPS, 2)),
        dma((STEPS, 4)), dma((STEPS, 4)),
        dma((STEPS,)), dma((STEPS,)),
        dma((STEPS,)), dma((STEPS,)),
    ]
    moved, speed, push = pl.pallas_call(
        kernel,
        out_shape=(out, out, out),
        in_specs=[hbm] * len(arguments),
        out_specs=(vmem, vmem, vmem),
        scratch_shapes=scratch,
        compiler_params=pltpu.CompilerParams(
            collective_id=0, has_side_effects=True, vmem_limit_bytes=56 * 1024 * 1024
        ),
        name="density_steps",
    )(*arguments)
    speed = speed + push
    return moved + TIME_STEP * speed, speed


def solution(mesh):
    return jax.shard_map(
        per_device,
        mesh=mesh,
        in_specs=(
            P("dom", None, "slab"),
            P(None, "dom", "slab", None),
            P(None, "dom", "slab", None),
            P("dom", "slab", None),
            P(None, "dom", "slab", None),
            P("dom", "slab", None, None),
            P("dom", "slab", None, None),
        ),
        out_specs=(P(None, "dom", "slab", None), P(None, "dom", "slab", None)),
        check_vma=False,
    )
```
